32 devices in a mesh: dp: 8 (over y, x, core), seq: 4 (over z).
Axes of the slice: x: 2, y: 2, z: 4, core: 2. Of those that a mesh axis runs over, the one named last changes fastest.
Arguments:
- queries: bfloat16 [8, 512, 2048], P('dp', 'seq'), may hold values from -5 to 5
- keys: bfloat16 [8, 512, 512], P('dp', 'seq'), may hold values from -5 to 5
- values: bfloat16 [8, 512, 512], P('dp', 'seq'), may hold values from -6 to 6
- upstream: bfloat16 [8, 512, 2048], P('dp', 'seq'), may hold values from -6 to 6
- doc_ids: int32 [8, 512], P('dp', 'seq'), may hold values from 0 to 11, never falling along the last dimension, each value on 1 to 64 neighbouring positions
Outputs:
- attended: bfloat16 [8, 512, 2048], P('dp', 'seq')
- query_grad: bfloat16 [8, 512, 2048], P('dp', 'seq')
- key_gradient: bfloat16 [8, 512, 512], P('dp', 'seq')
- value_gradient: bfloat16 [8, 512, 512], P('dp', 'seq')
The draws below stay inside these ranges and needn't reach their ends.
Inputs may be any that keep to these rules, and one draw needn't show every extreme that they name: `doc_ids`: in every row the document number never falls along the positions; each document holds at most 64 positions, and one holds exactly 64.
All inputs are finite; a program needn't handle non-finite values.
Results may differ from the reference program's by a relative error of at most 0.018.
Values may be sent and summed in bfloat16 or wider, within the bound.
A program may use at most 64 MiB of HBM per device.

```python
import math
import jax
import jax.numpy as jnp
import numpy as np
from jax import lax

QUERY_HEADS = 16
KEY_VALUE_HEADS = 4
HEAD_DIMENSION = 128
DOCS = 12
SLAB = 16
ROW_TOKENS = 512
DOC_MOST = 64
N_DP = 8
N_SEQ = 4


def draw_queries(key, part):
    key = jax.random.fold_in(key, 7)
    random_sample = jnp.clip(jax.random.normal(key, (N_DP, ROW_TOKENS, QUERY_HEADS * HEAD_DIMENSION), jnp.float32), -5.0, 5.0)
    return random_sample.astype(jnp.bfloat16)


def draw_keys(key, part):
    key = jax.random.fold_in(key, 13)
    random_sample = jnp.clip(jax.random.normal(key, (N_DP, ROW_TOKENS, KEY_VALUE_HEADS * HEAD_DIMENSION), jnp.float32), -5.0, 5.0)
    return random_sample.astype(jnp.bfloat16)


def block_levels(key, shape, shards, least, high):
    factor_of = 1.0
    for position, shards_of in shards:
        heights = jax.random.uniform(jax.random.fold_in(jax.random.fold_in(key, 6), position), (shards_of,), jnp.float32, least / len(shards), high / len(shards))
        factor_of = factor_of * jnp.repeat(jnp.exp(heights), shape[position] // shards_of).reshape((-1,) + (1,) * (len(shape) - 1 - position))
    return factor_of


def profile(number_of, total, most, lean):
    weights = [(1 << 20) // math.isqrt(rank ** lean) + 1 for rank in range(2, number_of + 1)]
    rest, holding = total - most - (number_of - 1), [1] * (number_of - 1)
    while rest > 0:
        free = [i for i in range(number_of - 1) if holding[i] < most]
        whole, left = sum([weights[i] for i in free]), rest
        for i in free:
            more = min(most - holding[i], max(1, left * weights[i] // whole), rest)
            holding[i] = holding[i] + more
            rest = rest - more
    return np.array([most] + holding)


def uneven_parts(stream_key, amount, total, limit, lean):
    if amount == 2:
        one = jax.random.randint(stream_key, (), max(1, total - limit), min(limit, total - 1) + 1)
        return jnp.stack([one, total - one])
    tallies = jnp.asarray(profile(amount, total, limit, lean), jnp.int32)
    couples = (amount - 1) // 2
    source_of, receiver = tallies[1:1 + 2 * couples:2], tallies[2:2 + 2 * couples:2]
    room = jnp.minimum(source_of - 1, limit - receiver)
    shifted = jax.random.randint(jax.random.fold_in(stream_key, 1), (couples,), 0, 1 << 20) % (room + 1)
    tallies = tallies.at[1:1 + 2 * couples:2].set(source_of - shifted).at[2:2 + 2 * couples:2].set(receiver + shifted)
    return tallies[jax.random.permutation(jax.random.fold_in(stream_key, 2), amount)]


def normal_values(rng, shape, width, bound, cuts=(), held_as=jnp.bfloat16):
    level = block_levels(rng, shape, cuts, -0.22, 0.18) if cuts else 1.0
    result = jax.random.normal(rng, shape, jnp.float32) * width * level
    return jnp.minimum(jnp.maximum(result, -bound), bound).astype(held_as)


def setup_inputs(seed: int = 0) -> dict:
    splits = jax.random.split(jax.random.key(seed), 6)
    queries = draw_queries(jax.random.fold_in(splits[5], 71), 0)
    keys = draw_keys(jax.random.fold_in(splits[5], 71), 0)
    values = normal_values(splits[2], (N_DP, ROW_TOKENS, KEY_VALUE_HEADS * HEAD_DIMENSION), 1.0, 6.0, ((0, 8), (1, 4)))
    upstream = normal_values(splits[3], (N_DP, ROW_TOKENS, QUERY_HEADS * HEAD_DIMENSION), 1.0, 6.0, ((0, 8), (1, 4)))
    doc_ids = jax.vmap(lambda own: jnp.searchsorted(jnp.cumsum(uneven_parts(own, DOCS, ROW_TOKENS, DOC_MOST, 2)), jnp.arange(ROW_TOKENS), side="right"))(jax.random.split(splits[4], N_DP)).reshape((N_DP, ROW_TOKENS)).astype(jnp.int32)
    return {"queries": queries, "keys": keys, "values": values, "upstream": upstream, "doc_ids": doc_ids}


def regroup(packed):
    features = packed.shape[-1]
    split_up = packed.reshape(N_DP, N_SEQ, N_DP, SLAB, features)
    return jnp.transpose(split_up, (2, 1, 0, 3, 4)).reshape(N_DP, ROW_TOKENS, features)

def one_head(operands):
    queries, keys, values, upstream, doc_row = operands
    scaling = 1.0 / math.sqrt(HEAD_DIMENSION)
    block_rows = min(512, ROW_TOKENS)
    positions = jnp.arange(ROW_TOKENS, dtype=jnp.int32)
    key_gradient = jnp.zeros((ROW_TOKENS, HEAD_DIMENSION), jnp.float32)
    value_gradient = jnp.zeros((ROW_TOKENS, HEAD_DIMENSION), jnp.float32)
    attended_parts = []
    query_parts = []
    for number in range(ROW_TOKENS // block_rows):
        start_row = number * block_rows
        finish = start_row + block_rows
        lowest = max(0, start_row - DOC_MOST)
        query_block = queries[start_row:finish]
        upstream_block = upstream[start_row:finish]
        key_part = keys[lowest:finish]
        value_part = values[lowest:finish]
        scores = jnp.dot(query_block, key_part.T, preferred_element_type=jnp.float32) * scaling
        allowed = (doc_row[None, lowest:finish] == doc_row[start_row:finish, None]) & (positions[None, lowest:finish] <= positions[start_row:finish, None])
        scores = jnp.where(allowed, scores, -jnp.inf)
        largest = lax.optimization_barrier(jnp.max(scores, axis=1, keepdims=True))
        weights = jnp.exp(scores - largest)
        normalized = weights / lax.optimization_barrier(jnp.sum(weights, axis=1, keepdims=True))
        probs_half = normalized.astype(jnp.bfloat16)
        attended_block = jnp.dot(probs_half, value_part, preferred_element_type=jnp.float32).astype(jnp.bfloat16)
        row_delta = lax.optimization_barrier(jnp.sum(upstream_block.astype(jnp.float32) * attended_block.astype(jnp.float32), axis=1, keepdims=True))
        prob_grad = jnp.dot(upstream_block, value_part.T, preferred_element_type=jnp.float32)
        score_grad = (normalized * (prob_grad - row_delta)).astype(jnp.bfloat16)
        query_parts.append((jnp.dot(score_grad, key_part, preferred_element_type=jnp.float32) * scaling).astype(jnp.bfloat16))
        key_gradient = key_gradient.at[lowest:finish].add(jnp.dot(score_grad.T, query_block, preferred_element_type=jnp.float32) * scaling)
        value_gradient = value_gradient.at[lowest:finish].add(jnp.dot(probs_half.T, upstream_block, preferred_element_type=jnp.float32))
        attended_parts.append(attended_block)
    return (jnp.concatenate(attended_parts), jnp.concatenate(query_parts), key_gradient, value_gradient)

def one_group(operands):
    query_group, keys, values, upstream_group, doc_row = operands

    def per_head(head_inputs):
        return one_head((head_inputs[0], keys, values, head_inputs[1], doc_row))
    attended, query_grad, key_gradient, value_gradient = lax.map(per_head, (query_group, upstream_group))
    return (attended, query_grad, lax.optimization_barrier(jnp.sum(key_gradient, axis=0)).astype(jnp.bfloat16), lax.optimization_barrier(jnp.sum(value_gradient, axis=0)).astype(jnp.bfloat16))

def one_row(operands):
    queries, keys, values, upstream, doc_row = operands
    queries_per_group = QUERY_HEADS // KEY_VALUE_HEADS
    query_head_array = queries.reshape(ROW_TOKENS, KEY_VALUE_HEADS, queries_per_group, HEAD_DIMENSION).transpose(1, 2, 0, 3)
    incoming_gradient_heads = upstream.reshape(ROW_TOKENS, KEY_VALUE_HEADS, queries_per_group, HEAD_DIMENSION).transpose(1, 2, 0, 3)
    key_head_array = keys.reshape(ROW_TOKENS, KEY_VALUE_HEADS, HEAD_DIMENSION).transpose(1, 0, 2)
    value_head_array = values.reshape(ROW_TOKENS, KEY_VALUE_HEADS, HEAD_DIMENSION).transpose(1, 0, 2)

    def per_group(group_inputs):
        return one_group((group_inputs[0], group_inputs[1], group_inputs[2], group_inputs[3], doc_row))
    attended, query_grad, key_gradient, value_gradient = lax.map(per_group, (query_head_array, key_head_array, value_head_array, incoming_gradient_heads))
    attended = attended.transpose(2, 0, 1, 3).reshape(ROW_TOKENS, QUERY_HEADS * HEAD_DIMENSION)
    query_grad = query_grad.transpose(2, 0, 1, 3).reshape(ROW_TOKENS, QUERY_HEADS * HEAD_DIMENSION)
    key_gradient = key_gradient.transpose(1, 0, 2).reshape(ROW_TOKENS, KEY_VALUE_HEADS * HEAD_DIMENSION)
    value_gradient = value_gradient.transpose(1, 0, 2).reshape(ROW_TOKENS, KEY_VALUE_HEADS * HEAD_DIMENSION)
    return (attended, query_grad, key_gradient, value_gradient)

def reference(queries, keys, values, upstream, doc_ids):
    attended, query_grad, key_gradient, value_gradient = lax.map(one_row, (regroup(queries), regroup(keys), regroup(values), regroup(upstream), doc_ids))
    return (regroup(attended), regroup(query_grad), regroup(key_gradient), regroup(value_gradient))
```

```python
import functools
import math

import jax
import jax.numpy as jnp
from jax import lax
from jax.experimental import pallas as pl
from jax.experimental.pallas import tpu as pltpu
from jax.sharding import PartitionSpec as P

QUERY_HEADS = 16
KEY_VALUE_HEADS = 4
HEAD_DIMENSION = 128


def attend(queries, keys, values, upstream, doc_row):
    seq_rows = queries.shape[0]
    scaling = 1.0 / math.sqrt(queries.shape[2])
    block_rows = min(512, seq_rows)
    longest = seq_rows // 8
    positions = lax.iota(jnp.int32, seq_rows)
    key_gradient = jnp.zeros(keys.shape, jnp.float32)
    value_gradient = jnp.zeros(values.shape, jnp.float32)
    attended_parts = []
    query_parts = []
    for number in range(seq_rows // block_rows):
        start_row = number * block_rows
        finish = start_row + block_rows
        lowest = max(0, start_row - longest)
        query_block = queries[start_row:finish]
        upstream_block = upstream[start_row:finish]
        key_part = keys[lowest:finish]
        value_part = values[lowest:finish]
        scores = (
            jnp.einsum("qhd,khd->hqk", query_block, key_part, preferred_element_type=jnp.float32)
            * scaling
        )
        allowed = (doc_row[None, lowest:finish] == doc_row[start_row:finish, None]) & (
            positions[None, lowest:finish] <= positions[start_row:finish, None]
        )
        scores = jnp.where(allowed[None], scores, -jnp.inf)
        largest = jnp.max(scores, axis=2, keepdims=True)
        weights = jnp.exp(scores - largest)
        normalized = weights / jnp.sum(weights, axis=2, keepdims=True)
        probs_half = normalized.astype(jnp.bfloat16)
        attended_block = jnp.einsum(
            "hqk,khd->qhd", probs_half, value_part, preferred_element_type=jnp.float32
        ).astype(jnp.bfloat16)
        row_delta = jnp.sum(
            upstream_block.astype(jnp.float32) * attended_block.astype(jnp.float32), axis=2
        ).T[:, :, None]
        prob_grad = jnp.einsum(
            "qhd,khd->hqk", upstream_block, value_part, preferred_element_type=jnp.float32
        )
        score_grad = (normalized * (prob_grad - row_delta)).astype(jnp.bfloat16)
        query_parts.append(
            (
                jnp.einsum("hqk,khd->qhd", score_grad, key_part, preferred_element_type=jnp.float32)
                * scaling
            ).astype(jnp.bfloat16)
        )
        key_gradient = key_gradient.at[lowest:finish].add(
            jnp.einsum("hqk,qhd->khd", score_grad, query_block, preferred_element_type=jnp.float32)
            * scaling
        )
        value_gradient = value_gradient.at[lowest:finish].add(
            jnp.einsum(
                "hqk,qhd->khd", probs_half, upstream_block, preferred_element_type=jnp.float32
            )
        )
        attended_parts.append(attended_block)
    return (
        jnp.concatenate(attended_parts),
        jnp.concatenate(query_parts),
        key_gradient,
        value_gradient,
    )


def shards(queries, keys, values, upstream, doc_ids):
    tokens_per_shard = queries.shape[1]
    group_count = lax.axis_size("dp")
    packed_slab_rows = tokens_per_shard // group_count
    head_local = QUERY_HEADS // lax.axis_size("seq")
    queries_per_group = QUERY_HEADS // KEY_VALUE_HEADS
    query_rows, key_row_array, value_row_array, upstream_rows = (
        lax.all_to_all(
            queries.reshape(group_count, packed_slab_rows, QUERY_HEADS * HEAD_DIMENSION),
            "dp",
            split_axis=0,
            concat_axis=0,
            tiled=True,
        ),
        lax.all_to_all(
            keys.reshape(group_count, packed_slab_rows, KEY_VALUE_HEADS * HEAD_DIMENSION),
            "dp",
            split_axis=0,
            concat_axis=0,
            tiled=True,
        ),
        lax.all_to_all(
            values.reshape(group_count, packed_slab_rows, KEY_VALUE_HEADS * HEAD_DIMENSION),
            "dp",
            split_axis=0,
            concat_axis=0,
            tiled=True,
        ),
        lax.all_to_all(
            upstream.reshape(group_count, packed_slab_rows, QUERY_HEADS * HEAD_DIMENSION),
            "dp",
            split_axis=0,
            concat_axis=0,
            tiled=True,
        ),
    )
    query_tok = query_rows.reshape(tokens_per_shard, QUERY_HEADS, HEAD_DIMENSION)
    upstream_tok = upstream_rows.reshape(tokens_per_shard, QUERY_HEADS, HEAD_DIMENSION)
    key_tokens = key_row_array.reshape(tokens_per_shard, KEY_VALUE_HEADS, HEAD_DIMENSION)
    value_tokens = value_row_array.reshape(tokens_per_shard, KEY_VALUE_HEADS, HEAD_DIMENSION)
    doc_row = lax.all_gather(doc_ids, "seq", axis=1, tiled=True)[0]
    query_head_array, incoming_gradient_heads = (
        lax.all_to_all(query_tok, "seq", split_axis=1, concat_axis=0, tiled=True),
        lax.all_to_all(upstream_tok, "seq", split_axis=1, concat_axis=0, tiled=True),
    )
    key_whole, value_whole = (
        lax.all_gather(key_tokens, "seq", axis=0, tiled=True),
        lax.all_gather(value_tokens, "seq", axis=0, tiled=True),
    )
    head_ids = (
        lax.axis_index("seq") * head_local + lax.iota(jnp.int32, head_local)
    ) // queries_per_group
    key_head_array = jnp.take(key_whole, head_ids, axis=1)
    value_head_array = jnp.take(value_whole, head_ids, axis=1)
    attended, query_grad, key_gradient, value_gradient = attend(
        query_head_array, key_head_array, value_head_array, incoming_gradient_heads, doc_row
    )
    attended_back, query_back = (
        lax.all_to_all(attended, "seq", split_axis=0, concat_axis=1, tiled=True),
        lax.all_to_all(query_grad, "seq", split_axis=0, concat_axis=1, tiled=True),
    )
    key_backward, value_backward = (
        lax.all_to_all(key_gradient, "seq", split_axis=0, concat_axis=1, tiled=True),
        lax.all_to_all(value_gradient, "seq", split_axis=0, concat_axis=1, tiled=True),
    )
    key_gradient_total = jnp.sum(
        key_backward.reshape(tokens_per_shard, KEY_VALUE_HEADS, queries_per_group, HEAD_DIMENSION),
        axis=2,
    ).astype(jnp.bfloat16)
    value_gradient_total = jnp.sum(
        value_backward.reshape(
            tokens_per_shard, KEY_VALUE_HEADS, queries_per_group, HEAD_DIMENSION
        ),
        axis=2,
    ).astype(jnp.bfloat16)
    attended_out, query_out, key_result, value_result = (
        lax.all_to_all(
            attended_back.reshape(group_count, packed_slab_rows, QUERY_HEADS * HEAD_DIMENSION),
            "dp",
            split_axis=0,
            concat_axis=0,
            tiled=True,
        ),
        lax.all_to_all(
            query_back.reshape(group_count, packed_slab_rows, QUERY_HEADS * HEAD_DIMENSION),
            "dp",
            split_axis=0,
            concat_axis=0,
            tiled=True,
        ),
        lax.all_to_all(
            key_gradient_total.reshape(
                group_count, packed_slab_rows, KEY_VALUE_HEADS * HEAD_DIMENSION
            ),
            "dp",
            split_axis=0,
            concat_axis=0,
            tiled=True,
        ),
        lax.all_to_all(
            value_gradient_total.reshape(
                group_count, packed_slab_rows, KEY_VALUE_HEADS * HEAD_DIMENSION
            ),
            "dp",
            split_axis=0,
            concat_axis=0,
            tiled=True,
        ),
    )
    return (
        attended_out.reshape(1, tokens_per_shard, QUERY_HEADS * HEAD_DIMENSION),
        query_out.reshape(1, tokens_per_shard, QUERY_HEADS * HEAD_DIMENSION),
        key_result.reshape(1, tokens_per_shard, KEY_VALUE_HEADS * HEAD_DIMENSION),
        value_result.reshape(1, tokens_per_shard, KEY_VALUE_HEADS * HEAD_DIMENSION),
    )


MESH = pl.DeviceIdType.MESH
SLAB = 16
ROWS = 8
CHUNKS = 4
CHUNK_ROWS = ROWS // CHUNKS
REACH = 2
SLOTS = 2 * REACH + 2
WINDOW = SLOTS * SLAB
HALF_Q = QUERY_HEADS * HEAD_DIMENSION // 2
HALF_K = KEY_VALUE_HEADS * HEAD_DIMENSION // 2
GROUP = QUERY_HEADS // KEY_VALUE_HEADS
SCALING = 1.0 / math.sqrt(HEAD_DIMENSION)
MASKED = -1e30


def kernel(
    n_dp, n_seq, q, k, v, u, doc, att, dq, dk, dv,
    qb, ub, kw, vw, ob, gb, kg, vg, kp, vp, ks, vs, docs, dwin, bias,
    doc_send, doc_recv, doc_local, fwd_send, fwd_recv, half_send, half_recv, local_in,
    back_send, back_recv, out_send, out_recv, local_out, final_out,
):
    d = lax.axis_index("dp")
    z = lax.axis_index("seq")
    chip, s = d // 2, d % 2
    chips = n_dp // 2
    place = z * chips + chip
    last = n_seq * chips - 1
    before, after = (z + n_seq - 1) % n_seq, (z + 1) % n_seq
    sibling = (chip * 2 + 1 - s, z)

    def remote(src, dst, send, recv, device):
        return pltpu.make_async_remote_copy(
            src_ref=src, dst_ref=dst, send_sem=send, recv_sem=recv,
            device_id=device, device_id_type=MESH,
        )

    def device_at(where, core):
        inside = (where + n_seq * chips) % (n_seq * chips)
        return ((inside % chips) * 2 + core, inside // chips)

    barrier = pltpu.get_barrier_semaphore()
    for step in range(1, n_dp):
        pl.semaphore_signal(barrier, inc=1, device_id=((d + step) % n_dp, z), device_id_type=MESH)

    @pl.when(z > 0)
    def _():
        for other in range(n_dp):
            pl.semaphore_signal(barrier, inc=1, device_id=(other, before), device_id_type=MESH)

    @pl.when(z < n_seq - 1)
    def _():
        for other in range(n_dp):
            pl.semaphore_signal(barrier, inc=1, device_id=(other, after), device_id_type=MESH)

    planes = (z > 0).astype(jnp.int32) + (z < n_seq - 1).astype(jnp.int32)
    own_cols = pl.ds(pl.multiple_of(s * HALF_Q, HALF_Q), HALF_Q)
    sib_cols = pl.ds(pl.multiple_of((1 - s) * HALF_Q, HALF_Q), HALF_Q)
    own_kcols = pl.ds(pl.multiple_of(s * HALF_K, HALF_K), HALF_K)
    sib_kcols = pl.ds(pl.multiple_of((1 - s) * HALF_K, HALF_K), HALF_K)

    def rows_of(chunk):
        return pl.ds(chunk * CHUNK_ROWS, CHUNK_ROWS)

    def local_in_copies(chunk):
        rows = rows_of(chunk)
        return [
            pltpu.make_async_copy(k.at[rows, :, own_kcols], kw.at[rows, 2 * REACH + s], local_in.at[chunk, 0]),
            pltpu.make_async_copy(v.at[rows, :, own_kcols], vw.at[rows, 2 * REACH + s], local_in.at[chunk, 1]),
            pltpu.make_async_copy(q.at[rows, :, own_cols], qb.at[rows, s], local_in.at[chunk, 2]),
            pltpu.make_async_copy(u.at[rows, :, own_cols], ub.at[rows, s], local_in.at[chunk, 3]),
        ]

    own_doc = pltpu.make_async_copy(doc, docs.at[n_dp + d], doc_local)
    own_doc.start()
    for chunk in range(CHUNKS):
        for copy in local_in_copies(chunk):
            copy.start()

    for offset in range(1, REACH + 1):

        @pl.when(place < offset)
        def _():
            for core in range(2):
                slot = 2 * (REACH - offset) + core
                kw[:, slot] = jnp.zeros((ROWS, SLAB, HALF_K), jnp.bfloat16)
                vw[:, slot] = jnp.zeros((ROWS, SLAB, HALF_K), jnp.bfloat16)

        @pl.when(place + offset > last)
        def _():
            kp[offset] = jnp.zeros((ROWS, SLAB, 2 * HALF_K), jnp.bfloat16)
            vp[offset] = jnp.zeros((ROWS, SLAB, 2 * HALF_K), jnp.bfloat16)

    @pl.when(z == 0)
    def _():
        docs[0:n_dp] = jnp.zeros((n_dp, 1, n_dp * SLAB), jnp.int32)

    pl.semaphore_wait(barrier, n_dp - 1 + n_dp * planes)

    def doc_near(step):
        return remote(
            doc, docs.at[n_dp + d], doc_send.at[step], doc_recv.at[n_dp + d], ((d + step) % n_dp, z)
        )

    def doc_next(other):
        return remote(
            doc, docs.at[d], doc_send.at[n_dp + other], doc_recv.at[d], (other, after)
        )

    for step in range(1, n_dp):
        doc_near(step).start()

    @pl.when(z < n_seq - 1)
    def _():
        for other in range(n_dp):
            doc_next(other).start()

    def forward(chunk, kind, offset, core):
        src, dst = ((k, kw), (v, vw))[kind]
        rows = rows_of(chunk)
        columns = pl.ds(core * HALF_K, HALF_K)
        return remote(
            src.at[rows, :, columns],
            dst.at[rows, 2 * (REACH - offset) + s],
            fwd_send.at[chunk, kind, 2 * offset + core],
            fwd_recv.at[chunk, kind, 2 * (REACH - offset) + s],
            device_at(place + offset, core),
        )

    def forward_sibling(chunk, kind):
        src, dst = ((k, kw), (v, vw))[kind]
        rows = rows_of(chunk)
        return remote(
            src.at[rows, :, sib_kcols],
            dst.at[rows, 2 * REACH + s],
            fwd_send.at[chunk, kind, 0],
            fwd_recv.at[chunk, kind, 2 * REACH + s],
            sibling,
        )

    def half_over(chunk, kind):
        src, dst = ((q, qb), (u, ub))[kind]
        rows = rows_of(chunk)
        return remote(
            src.at[rows, :, sib_cols], dst.at[rows, s],
            half_send.at[chunk, kind], half_recv.at[chunk, kind], sibling,
        )

    def send_forward(chunk, act):
        for offset in range(REACH, 0, -1):

            @pl.when(place + offset <= last)
            def _():
                for kind in range(2):
                    for core in range(2):
                        act(forward(chunk, kind, offset, core))

        for kind in range(2):
            act(forward_sibling(chunk, kind))
            act(half_over(chunk, kind))

    for chunk in range(CHUNKS):
        send_forward(chunk, lambda copy: copy.start())

    own_doc.wait()
    for step in range(1, n_dp):
        other = (d + step) % n_dp
        pltpu.make_async_copy(doc, docs.at[n_dp + other], doc_recv.at[n_dp + other]).wait()

    @pl.when(z > 0)
    def _():
        for other in range(n_dp):
            pltpu.make_async_copy(doc, docs.at[other], doc_recv.at[other]).wait()

    for row in range(n_dp):
        dwin[row : row + 1, 0:128] = docs[row]
        dwin[row : row + 1, 128:256] = docs[n_dp + row]
    lead = 128 - 2 * REACH * SLAB
    both = dwin[...]
    window = jnp.zeros((n_dp, 128), jnp.int32)
    for candidate in range(chips):
        begin = lead + candidate * 2 * SLAB
        shifted = pltpu.roll(both, 256 - begin, axis=1)[:, :128]
        window = jnp.where(chip == candidate, shifted, window)
    own = window[:, 2 * REACH * SLAB : WINDOW]
    query_docs = jnp.concatenate([own] * GROUP, axis=1)
    key_docs = window.astype(jnp.float32).T[:WINDOW]
    key_at = lax.broadcasted_iota(jnp.int32, (WINDOW, 128), 0)
    query_at = lax.broadcasted_iota(jnp.int32, (WINDOW, 128), 1) % (2 * SLAB) + 2 * REACH * SLAB
    in_order = (key_at <= query_at) & (key_at >= 2 * REACH * SLAB - place * 2 * SLAB)
    query_docs = query_docs.astype(jnp.float32)
    for row in range(n_dp):
        same = key_docs[:, row : row + 1] == query_docs[row : row + 1, :]
        bias[row] = jnp.where(same & in_order, 0.0, MASKED)

    def backward(chunk, kind, offset, core):
        src, dst = ((kg, kp), (vg, vp))[kind]
        rows = rows_of(chunk)
        return remote(
            src.at[rows, 2 * (REACH - offset) + core],
            dst.at[offset, rows, :, own_kcols],
            back_send.at[chunk, kind, 2 * offset + core],
            back_recv.at[chunk, kind, 2 * offset + s],
            device_at(place - offset, core),
        )

    def backward_sibling(chunk, kind):
        src, dst = ((kg, kp), (vg, vp))[kind]
        rows = rows_of(chunk)
        return remote(
            src.at[rows, 2 * REACH + 1 - s],
            dst.at[0, rows, :, own_kcols],
            back_send.at[chunk, kind, 0],
            back_recv.at[chunk, kind, s],
            sibling,
        )

    def out_over(chunk, kind):
        src, dst = ((ob, att), (gb, dq))[kind]
        rows = rows_of(chunk)
        return remote(
            src.at[rows, 1 - s], dst.at[rows, :, own_cols],
            out_send.at[chunk, kind], out_recv.at[chunk, kind], sibling,
        )

    def local_out_copy(chunk, which):
        rows = rows_of(chunk)
        if which < 2:
            src, dst = ((kg, kp), (vg, vp))[which]
            return pltpu.make_async_copy(
                src.at[rows, 2 * REACH + s], dst.at[0, rows, :, own_kcols], local_out.at[chunk, which]
            )
        src, dst = ((ob, att), (gb, dq))[which - 2]
        return pltpu.make_async_copy(
            src.at[rows, s], dst.at[rows, :, own_cols], local_out.at[chunk, which]
        )

    def send_backward(chunk, act):
        for offset in range(REACH, 0, -1):

            @pl.when(place - offset >= 0)
            def _():
                for kind in range(2):
                    for core in range(2):
                        act(backward(chunk, kind, offset, core))

        for kind in range(2):
            act(backward_sibling(chunk, kind))
            act(out_over(chunk, kind))

    def await_inputs(chunk):
        rows = rows_of(chunk)
        for copy in local_in_copies(chunk):
            copy.wait()
        for kind in range(2):
            src, dst = ((k, kw), (v, vw))[kind]
            slot = 2 * REACH + 1 - s
            pltpu.make_async_copy(
                src.at[rows, :, own_kcols], dst.at[rows, slot], fwd_recv.at[chunk, kind, slot]
            ).wait()
            src, dst = ((q, qb), (u, ub))[kind]
            pltpu.make_async_copy(
                src.at[rows, :, own_cols], dst.at[rows, 1 - s], half_recv.at[chunk, kind]
            ).wait()
        for offset in range(1, REACH + 1):

            @pl.when(place >= offset)
            def _():
                for kind in range(2):
                    src, dst = ((k, kw), (v, vw))[kind]
                    for core in range(2):
                        slot = 2 * (REACH - offset) + core
                        pltpu.make_async_copy(
                            src.at[rows, :, own_kcols], dst.at[rows, slot], fwd_recv.at[chunk, kind, slot]
                        ).wait()

    def dot(a, b, dims):
        return lax.dot_general(a, b, (dims, ((), ())), preferred_element_type=jnp.float32)

    def compute(chunk):
        tasks = [(i, g) for i in range(CHUNK_ROWS) for g in range(2)]
        first = chunk * CHUNK_ROWS

        def stacked(ref, i, g):
            parts = []
            for h in range(GROUP):
                at = (g * GROUP + h) * HEAD_DIMENSION
                parts.append(ref[first + i, :, :, at : at + HEAD_DIMENSION].reshape(2 * SLAB, HEAD_DIMENSION))
            return jnp.concatenate(parts, axis=0)

        def windowed(ref, i, g):
            at = g * HEAD_DIMENSION
            return ref[first + i, :, :, at : at + HEAD_DIMENSION].reshape(WINDOW, HEAD_DIMENSION)

        def spread(ref, i, g, value):
            for h in range(GROUP):
                at = (g * GROUP + h) * HEAD_DIMENSION
                part = value[h * 2 * SLAB : (h + 1) * 2 * SLAB].astype(jnp.bfloat16)
                ref[first + i, :, :, at : at + HEAD_DIMENSION] = part.reshape(2, SLAB, HEAD_DIMENSION)

        def unwindow(ref, i, g, value):
            at = g * HEAD_DIMENSION
            ref[first + i, :, :, at : at + HEAD_DIMENSION] = value.astype(jnp.bfloat16).reshape(
                SLOTS, SLAB, HEAD_DIMENSION
            )

        scores = [dot(windowed(kw, i, g), stacked(qb, i, g), ((1,), (1,))) for i, g in tasks]
        prob_grads = [dot(windowed(vw, i, g), stacked(ub, i, g), ((1,), (1,))) for i, g in tasks]
        probs, grads = [], []
        for (i, g), score, prob_grad in zip(tasks, scores, prob_grads):
            score = score * SCALING + bias[first + i]
            weights = jnp.exp(score - jnp.max(score, axis=0, keepdims=True))
            normalized = weights / jnp.sum(weights, axis=0, keepdims=True)
            delta = jnp.sum(normalized * prob_grad, axis=0, keepdims=True)
            probs.append(normalized.astype(jnp.bfloat16))
            grads.append((normalized * (prob_grad - delta)).astype(jnp.bfloat16))
        for (i, g), prob, grad in zip(tasks, probs, grads):
            unwindow(kg, i, g, dot(grad, stacked(qb, i, g), ((1,), (0,))) * SCALING)
            unwindow(vg, i, g, dot(prob, stacked(ub, i, g), ((1,), (0,))))
        for (i, g), prob, grad in zip(tasks, probs, grads):
            spread(ob, i, g, dot(prob, windowed(vw, i, g), ((0,), (0,))))
            spread(gb, i, g, dot(grad, windowed(kw, i, g), ((0,), (0,))) * SCALING)

    def step(chunk, carry):
        await_inputs(chunk)
        compute(chunk)
        send_backward(chunk, lambda copy: copy.start())
        for which in range(4):
            local_out_copy(chunk, which).start()
        return carry

    lax.fori_loop(0, CHUNKS, step, 0)

    def finish(chunk, carry):
        rows = rows_of(chunk)
        for kind in range(2):
            local_out_copy(chunk, kind).wait()
            src, dst = ((kg, kp), (vg, vp))[kind]
            pltpu.make_async_copy(
                src.at[rows, 2 * REACH + 1 - s], dst.at[0, rows, :, sib_kcols], back_recv.at[chunk, kind, 1 - s]
            ).wait()
        for offset in range(1, REACH + 1):

            @pl.when(place + offset <= last)
            def _():
                for kind in range(2):
                    src, dst = ((kg, kp), (vg, vp))[kind]
                    for core in range(2):
                        pltpu.make_async_copy(
                            src.at[rows, 2 * REACH],
                            dst.at[offset, rows, :, pl.ds(core * HALF_K, HALF_K)],
                            back_recv.at[chunk, kind, 2 * offset + core],
                        ).wait()

        for part, total, target, kind in ((kp, ks, dk, 0), (vp, vs, dv, 1)):
            value = part[0, rows].astype(jnp.float32)
            for offset in range(1, REACH + 1):
                value += part[offset, rows].astype(jnp.float32)
            total[rows] = value.astype(jnp.bfloat16)
            pltpu.make_async_copy(total.at[rows], target.at[rows], final_out.at[chunk, kind]).start()
        return carry

    lax.fori_loop(0, CHUNKS, finish, 0)

    for step in range(1, n_dp):
        doc_near(step).wait_send()

    @pl.when(z < n_seq - 1)
    def _():
        for other in range(n_dp):
            doc_next(other).wait_send()

    def drain(chunk, carry):
        rows = rows_of(chunk)
        send_forward(chunk, lambda copy: copy.wait_send())
        send_backward(chunk, lambda copy: copy.wait_send())
        for kind in range(2):
            src, dst = ((ob, att), (gb, dq))[kind]
            pltpu.make_async_copy(
                src.at[rows, s], dst.at[rows, :, sib_cols], out_recv.at[chunk, kind]
            ).wait()
            local_out_copy(chunk, 2 + kind).wait()
            total, target = ((ks, dk), (vs, dv))[kind]
            pltpu.make_async_copy(total.at[rows], target.at[rows], final_out.at[chunk, kind]).wait()
        return carry

    lax.fori_loop(0, CHUNKS, drain, 0)


def direct(n_dp, n_seq, queries, keys, values, upstream, doc_ids):
    wide = (ROWS, SLAB, QUERY_HEADS * HEAD_DIMENSION)
    narrow = (ROWS, SLAB, KEY_VALUE_HEADS * HEAD_DIMENSION)
    half = jnp.bfloat16
    anywhere = pl.BlockSpec(memory_space=pl.ANY)
    dma = pltpu.SemaphoreType.DMA
    results = pl.pallas_call(
        functools.partial(kernel, n_dp, n_seq),
        out_shape=[jax.ShapeDtypeStruct(shape, half) for shape in (wide, wide, narrow, narrow)],
        in_specs=[anywhere] * 5,
        out_specs=[anywhere] * 4,
        scratch_shapes=[
            pltpu.VMEM((ROWS, 2, SLAB, HALF_Q), half),
            pltpu.VMEM((ROWS, 2, SLAB, HALF_Q), half),
            pltpu.VMEM((ROWS, SLOTS, SLAB, HALF_K), half),
            pltpu.VMEM((ROWS, SLOTS, SLAB, HALF_K), half),
            pltpu.VMEM((ROWS, 2, SLAB, HALF_Q), half),
            pltpu.VMEM((ROWS, 2, SLAB, HALF_Q), half),
            pltpu.VMEM((ROWS, SLOTS, SLAB, HALF_K), half),
            pltpu.VMEM((ROWS, SLOTS, SLAB, HALF_K), half),
            pltpu.VMEM((REACH + 1,) + narrow, half),
            pltpu.VMEM((REACH + 1,) + narrow, half),
            pltpu.VMEM(narrow, half),
            pltpu.VMEM(narrow, half),
            pltpu.VMEM((2 * n_dp, 1, n_dp * SLAB), jnp.int32),
            pltpu.VMEM((n_dp, 2 * n_dp * SLAB), jnp.int32),
            pltpu.VMEM((ROWS, WINDOW, 128), jnp.float32),
            dma((2 * n_dp,)),
            dma((2 * n_dp,)),
            dma(()),
            dma((CHUNKS, 2, SLOTS)),
            dma((CHUNKS, 2, SLOTS)),
            dma((CHUNKS, 2)),
            dma((CHUNKS, 2)),
            dma((CHUNKS, 4)),
            dma((CHUNKS, 2, SLOTS)),
            dma((CHUNKS, 2, SLOTS)),
            dma((CHUNKS, 2)),
            dma((CHUNKS, 2)),
            dma((CHUNKS, 4)),
            dma((CHUNKS, 2)),
        ],
        compiler_params=pltpu.CompilerParams(
            collective_id=0, has_side_effects=True, vmem_limit_bytes=48 * 1024 * 1024
        ),
        cost_estimate=pl.CostEstimate(flops=10**9, bytes_accessed=10**7, transcendentals=10**6),
    )(
        queries.reshape(wide), keys.reshape(narrow), values.reshape(narrow),
        upstream.reshape(wide), doc_ids,
    )
    tokens = ROWS * SLAB
    return tuple(array.reshape(1, tokens, array.shape[-1]) for array in results)


def arranged(n_dp, n_seq, queries, keys, values, upstream, doc_ids):
    tokens = queries.shape[1]
    slab = tokens // n_dp
    longest = n_seq * tokens // 8
    if n_dp == ROWS and slab == SLAB and longest <= 2 * REACH * SLAB:
        return direct(n_dp, n_seq, queries, keys, values, upstream, doc_ids)
    return shards(queries, keys, values, upstream, doc_ids)


def pick(mesh):
    return functools.partial(arranged, mesh.shape["dp"], mesh.shape["seq"])


def solution(mesh):
    in_specs = (
        P("dp", "seq", None),
        P("dp", "seq", None),
        P("dp", "seq", None),
        P("dp", "seq", None),
        P("dp", "seq"),
    )
    out_specs = (
        P("dp", "seq", None),
        P("dp", "seq", None),
        P("dp", "seq", None),
        P("dp", "seq", None),
    )
    return jax.shard_map(
        pick(mesh), mesh=mesh, in_specs=in_specs, out_specs=out_specs, check_vma=False)
```

```python
import functools
import math

import jax
import jax.numpy as jnp
from jax import lax
from jax.experimental import pallas as pl
from jax.experimental.pallas import tpu as pltpu
from jax.sharding import PartitionSpec as P

QUERY_HEADS = 16
KEY_VALUE_HEADS = 4
HEAD_DIMENSION = 128


def attend(queries, keys, values, upstream, doc_row):
    seq_rows = queries.shape[0]
    scaling = 1.0 / math.sqrt(queries.shape[2])
    block_rows = min(512, seq_rows)
    longest = seq_rows // 8
    positions = lax.iota(jnp.int32, seq_rows)
    key_gradient = jnp.zeros(keys.shape, jnp.float32)
    value_gradient = jnp.zeros(values.shape, jnp.float32)
    attended_parts = []
    query_parts = []
    for number in range(seq_rows // block_rows):
        start_row = number * block_rows
        finish = start_row + block_rows
        lowest = max(0, start_row - longest)
        query_block = queries[start_row:finish]
        upstream_block = upstream[start_row:finish]
        key_part = keys[lowest:finish]
        value_part = values[lowest:finish]
        scores = (
            jnp.einsum("qhd,khd->hqk", query_block, key_part, preferred_element_type=jnp.float32)
            * scaling
        )
        allowed = (doc_row[None, lowest:finish] == doc_row[start_row:finish, None]) & (
            positions[None, lowest:finish] <= positions[start_row:finish, None]
        )
        scores = jnp.where(allowed[None], scores, -jnp.inf)
        largest = jnp.max(scores, axis=2, keepdims=True)
        weights = jnp.exp(scores - largest)
        normalized = weights / jnp.sum(weights, axis=2, keepdims=True)
        probs_half = normalized.astype(jnp.bfloat16)
        attended_block = jnp.einsum(
            "hqk,khd->qhd", probs_half, value_part, preferred_element_type=jnp.float32
        ).astype(jnp.bfloat16)
        row_delta = jnp.sum(
            upstream_block.astype(jnp.float32) * attended_block.astype(jnp.float32), axis=2
        ).T[:, :, None]
        prob_grad = jnp.einsum(
            "qhd,khd->hqk", upstream_block, value_part, preferred_element_type=jnp.float32
        )
        score_grad = (normalized * (prob_grad - row_delta)).astype(jnp.bfloat16)
        query_parts.append(
            (
                jnp.einsum("hqk,khd->qhd", score_grad, key_part, preferred_element_type=jnp.float32)
                * scaling
            ).astype(jnp.bfloat16)
        )
        key_gradient = key_gradient.at[lowest:finish].add(
            jnp.einsum("hqk,qhd->khd", score_grad, query_block, preferred_element_type=jnp.float32)
            * scaling
        )
        value_gradient = value_gradient.at[lowest:finish].add(
            jnp.einsum(
                "hqk,qhd->khd", probs_half, upstream_block, preferred_element_type=jnp.float32
            )
        )
        attended_parts.append(attended_block)
    return (
        jnp.concatenate(attended_parts),
        jnp.concatenate(query_parts),
        key_gradient,
        value_gradient,
    )


def shards(queries, keys, values, upstream, doc_ids):
    tokens_per_shard = queries.shape[1]
    group_count = lax.axis_size("dp")
    packed_slab_rows = tokens_per_shard // group_count
    head_local = QUERY_HEADS // lax.axis_size("seq")
    queries_per_group = QUERY_HEADS // KEY_VALUE_HEADS
    query_rows, key_row_array, value_row_array, upstream_rows = (
        lax.all_to_all(
            queries.reshape(group_count, packed_slab_rows, QUERY_HEADS * HEAD_DIMENSION),
            "dp",
            split_axis=0,
            concat_axis=0,
            tiled=True,
        ),
        lax.all_to_all(
            keys.reshape(group_count, packed_slab_rows, KEY_VALUE_HEADS * HEAD_DIMENSION),
            "dp",
            split_axis=0,
            concat_axis=0,
            tiled=True,
        ),
        lax.all_to_all(
            values.reshape(group_count, packed_slab_rows, KEY_VALUE_HEADS * HEAD_DIMENSION),
            "dp",
            split_axis=0,
            concat_axis=0,
            tiled=True,
        ),
        lax.all_to_all(
            upstream.reshape(group_count, packed_slab_rows, QUERY_HEADS * HEAD_DIMENSION),
            "dp",
            split_axis=0,
            concat_axis=0,
            tiled=True,
        ),
    )
    query_tok = query_rows.reshape(tokens_per_shard, QUERY_HEADS, HEAD_DIMENSION)
    upstream_tok = upstream_rows.reshape(tokens_per_shard, QUERY_HEADS, HEAD_DIMENSION)
    key_tokens = key_row_array.reshape(tokens_per_shard, KEY_VALUE_HEADS, HEAD_DIMENSION)
    value_tokens = value_row_array.reshape(tokens_per_shard, KEY_VALUE_HEADS, HEAD_DIMENSION)
    doc_row = lax.all_gather(doc_ids, "seq", axis=1, tiled=True)[0]
    query_head_array, incoming_gradient_heads = (
        lax.all_to_all(query_tok, "seq", split_axis=1, concat_axis=0, tiled=True),
        lax.all_to_all(upstream_tok, "seq", split_axis=1, concat_axis=0, tiled=True),
    )
    key_whole, value_whole = (
        lax.all_gather(key_tokens, "seq", axis=0, tiled=True),
        lax.all_gather(value_tokens, "seq", axis=0, tiled=True),
    )
    head_ids = (
        lax.axis_index("seq") * head_local + lax.iota(jnp.int32, head_local)
    ) // queries_per_group
    key_head_array = jnp.take(key_whole, head_ids, axis=1)
    value_head_array = jnp.take(value_whole, head_ids, axis=1)
    attended, query_grad, key_gradient, value_gradient = attend(
        query_head_array, key_head_array, value_head_array, incoming_gradient_heads, doc_row
    )
    attended_back, query_back = (
        lax.all_to_all(attended, "seq", split_axis=0, concat_axis=1, tiled=True),
        lax.all_to_all(query_grad, "seq", split_axis=0, concat_axis=1, tiled=True),
    )
    key_backward, value_backward = (
        lax.all_to_all(key_gradient, "seq", split_axis=0, concat_axis=1, tiled=True),
        lax.all_to_all(value_gradient, "seq", split_axis=0, concat_axis=1, tiled=True),
    )
    key_gradient_total = jnp.sum(
        key_backward.reshape(tokens_per_shard, KEY_VALUE_HEADS, queries_per_group, HEAD_DIMENSION),
        axis=2,
    ).astype(jnp.bfloat16)
    value_gradient_total = jnp.sum(
        value_backward.reshape(
            tokens_per_shard, KEY_VALUE_HEADS, queries_per_group, HEAD_DIMENSION
        ),
        axis=2,
    ).astype(jnp.bfloat16)
    attended_out, query_out, key_result, value_result = (
        lax.all_to_all(
            attended_back.reshape(group_count, packed_slab_rows, QUERY_HEADS * HEAD_DIMENSION),
            "dp",
            split_axis=0,
            concat_axis=0,
            tiled=True,
        ),
        lax.all_to_all(
            query_back.reshape(group_count, packed_slab_rows, QUERY_HEADS * HEAD_DIMENSION),
            "dp",
            split_axis=0,
            concat_axis=0,
            tiled=True,
        ),
        lax.all_to_all(
            key_gradient_total.reshape(
                group_count, packed_slab_rows, KEY_VALUE_HEADS * HEAD_DIMENSION
            ),
            "dp",
            split_axis=0,
            concat_axis=0,
            tiled=True,
        ),
        lax.all_to_all(
            value_gradient_total.reshape(
                group_count, packed_slab_rows, KEY_VALUE_HEADS * HEAD_DIMENSION
            ),
            "dp",
            split_axis=0,
            concat_axis=0,
            tiled=True,
        ),
    )
    return (
        attended_out.reshape(1, tokens_per_shard, QUERY_HEADS * HEAD_DIMENSION),
        query_out.reshape(1, tokens_per_shard, QUERY_HEADS * HEAD_DIMENSION),
        key_result.reshape(1, tokens_per_shard, KEY_VALUE_HEADS * HEAD_DIMENSION),
        value_result.reshape(1, tokens_per_shard, KEY_VALUE_HEADS * HEAD_DIMENSION),
    )


MESH = pl.DeviceIdType.MESH
SLAB = 16
ROWS = 8
CHUNKS = 4
AHEAD = 2
CHUNK_ROWS = ROWS // CHUNKS
REACH = 2
SLOTS = 2 * REACH + 2
WINDOW = SLOTS * SLAB
HALF_Q = QUERY_HEADS * HEAD_DIMENSION // 2
HALF_K = KEY_VALUE_HEADS * HEAD_DIMENSION // 2
GROUP = QUERY_HEADS // KEY_VALUE_HEADS
SCALING = 1.0 / math.sqrt(HEAD_DIMENSION)
MASKED = -1e30


def kernel(
    n_dp, n_seq, q_in, k_in, v_in, u_in, doc_in, att, dq, dk, dv,
    q, k, v, u, doc, qb, ub, kw, vw, ob, gb, kg, vg, kp, vp, ks, vs, docs, dwin, bias,
    staged, doc_send, doc_recv, doc_local, fwd_send, fwd_recv, half_send, half_recv, local_in,
    back_send, back_recv, out_send, out_recv, local_out, final_out,
):
    d = lax.axis_index("dp")
    z = lax.axis_index("seq")
    chip, s = d // 2, d % 2
    chips = n_dp // 2
    place = z * chips + chip
    last = n_seq * chips - 1
    before, after = (z + n_seq - 1) % n_seq, (z + 1) % n_seq
    sibling = (chip * 2 + 1 - s, z)

    def remote(src, dst, send, recv, device):
        return pltpu.make_async_remote_copy(
            src_ref=src, dst_ref=dst, send_sem=send, recv_sem=recv,
            device_id=device, device_id_type=MESH,
        )

    def device_at(where, core):
        inside = (where + n_seq * chips) % (n_seq * chips)
        return ((inside % chips) * 2 + core, inside // chips)

    stages = [
        pltpu.make_async_copy(src, dst, staged.at[i])
        for i, (src, dst) in enumerate(((doc_in, doc), (k_in, k), (v_in, v), (q_in, q), (u_in, u)))
    ]
    for copy in stages:
        copy.start()

    barrier = pltpu.get_barrier_semaphore()
    for step in range(1, n_dp):
        pl.semaphore_signal(barrier, inc=1, device_id=((d + step) % n_dp, z), device_id_type=MESH)

    @pl.when(z > 0)
    def _():
        for other in range(n_dp):
            pl.semaphore_signal(barrier, inc=1, device_id=(other, before), device_id_type=MESH)

    @pl.when(z < n_seq - 1)
    def _():
        for other in range(n_dp):
            pl.semaphore_signal(barrier, inc=1, device_id=(other, after), device_id_type=MESH)

    planes = (z > 0).astype(jnp.int32) + (z < n_seq - 1).astype(jnp.int32)
    own_cols = pl.ds(pl.multiple_of(s * HALF_Q, HALF_Q), HALF_Q)
    sib_cols = pl.ds(pl.multiple_of((1 - s) * HALF_Q, HALF_Q), HALF_Q)
    own_kcols = pl.ds(pl.multiple_of(s * HALF_K, HALF_K), HALF_K)
    sib_kcols = pl.ds(pl.multiple_of((1 - s) * HALF_K, HALF_K), HALF_K)

    def rows_of(chunk):
        return pl.ds(chunk * CHUNK_ROWS, CHUNK_ROWS)

    def local_in_copies(chunk):
        rows = rows_of(chunk)
        return [
            pltpu.make_async_copy(k.at[rows, :, own_kcols], kw.at[rows, 2 * REACH + s], local_in.at[chunk, 0]),
            pltpu.make_async_copy(v.at[rows, :, own_kcols], vw.at[rows, 2 * REACH + s], local_in.at[chunk, 1]),
            pltpu.make_async_copy(q.at[rows, :, own_cols], qb.at[rows, s], local_in.at[chunk, 2]),
            pltpu.make_async_copy(u.at[rows, :, own_cols], ub.at[rows, s], local_in.at[chunk, 3]),
        ]

    for offset in range(1, REACH + 1):

        @pl.when(place < offset)
        def _():
            for core in range(2):
                slot = 2 * (REACH - offset) + core
                kw[:, slot] = jnp.zeros((ROWS, SLAB, HALF_K), jnp.bfloat16)
                vw[:, slot] = jnp.zeros((ROWS, SLAB, HALF_K), jnp.bfloat16)

        @pl.when(place + offset > last)
        def _():
            kp[offset] = jnp.zeros((ROWS, SLAB, 2 * HALF_K), jnp.bfloat16)
            vp[offset] = jnp.zeros((ROWS, SLAB, 2 * HALF_K), jnp.bfloat16)

    @pl.when(z == 0)
    def _():
        docs[0:n_dp] = jnp.zeros((n_dp, 1, n_dp * SLAB), jnp.int32)

    pl.semaphore_wait(barrier, n_dp - 1 + n_dp * planes)

    stages[0].wait()
    own_doc = pltpu.make_async_copy(doc, docs.at[n_dp + d], doc_local)
    own_doc.start()

    def doc_near(step):
        return remote(
            doc, docs.at[n_dp + d], doc_send.at[step], doc_recv.at[n_dp + d], ((d + step) % n_dp, z)
        )

    def doc_next(other):
        return remote(
            doc, docs.at[d], doc_send.at[n_dp + other], doc_recv.at[d], (other, after)
        )

    for step in range(1, n_dp):
        doc_near(step).start()

    @pl.when(z < n_seq - 1)
    def _():
        for other in range(n_dp):
            doc_next(other).start()

    def forward(chunk, kind, offset, core):
        src, dst = ((k, kw), (v, vw))[kind]
        rows = rows_of(chunk)
        columns = pl.ds(core * HALF_K, HALF_K)
        return remote(
            src.at[rows, :, columns],
            dst.at[rows, 2 * (REACH - offset) + s],
            fwd_send.at[chunk, kind, 2 * offset + core],
            fwd_recv.at[chunk, kind, 2 * (REACH - offset) + s],
            device_at(place + offset, core),
        )

    def forward_sibling(chunk, kind):
        src, dst = ((k, kw), (v, vw))[kind]
        rows = rows_of(chunk)
        return remote(
            src.at[rows, :, sib_kcols],
            dst.at[rows, 2 * REACH + s],
            fwd_send.at[chunk, kind, 0],
            fwd_recv.at[chunk, kind, 2 * REACH + s],
            sibling,
        )

    def half_over(chunk, kind):
        src, dst = ((q, qb), (u, ub))[kind]
        rows = rows_of(chunk)
        return remote(
            src.at[rows, :, sib_cols], dst.at[rows, s],
            half_send.at[chunk, kind], half_recv.at[chunk, kind], sibling,
        )

    def send_forward(chunk, act):
        for offset in range(REACH, 0, -1):

            @pl.when(place + offset <= last)
            def _():
                for kind in range(2):
                    for core in range(2):
                        act(forward(chunk, kind, offset, core))

        for kind in range(2):
            act(forward_sibling(chunk, kind))
            act(half_over(chunk, kind))

    for copy in stages[1:]:
        copy.wait()
    for chunk in range(CHUNKS):
        for copy in local_in_copies(chunk):
            copy.start()
    for chunk in range(AHEAD):
        send_forward(chunk, lambda copy: copy.start())

    own_doc.wait()
    for step in range(1, n_dp):
        other = (d + step) % n_dp
        pltpu.make_async_copy(doc, docs.at[n_dp + other], doc_recv.at[n_dp + other]).wait()

    @pl.when(z > 0)
    def _():
        for other in range(n_dp):
            pltpu.make_async_copy(doc, docs.at[other], doc_recv.at[other]).wait()

    for row in range(n_dp):
        dwin[row : row + 1, 0:128] = docs[row]
        dwin[row : row + 1, 128:256] = docs[n_dp + row]
    lead = 128 - 2 * REACH * SLAB
    both = dwin[...]
    window = jnp.zeros((n_dp, 128), jnp.int32)
    for candidate in range(chips):
        begin = lead + candidate * 2 * SLAB
        shifted = pltpu.roll(both, 256 - begin, axis=1)[:, :128]
        window = jnp.where(chip == candidate, shifted, window)
    own = window[:, 2 * REACH * SLAB : WINDOW]
    query_docs = jnp.concatenate([own] * GROUP, axis=1)
    key_docs = window.astype(jnp.float32).T[:WINDOW]
    key_at = lax.broadcasted_iota(jnp.int32, (WINDOW, 128), 0)
    query_at = lax.broadcasted_iota(jnp.int32, (WINDOW, 128), 1) % (2 * SLAB) + 2 * REACH * SLAB
    in_order = (key_at <= query_at) & (key_at >= 2 * REACH * SLAB - place * 2 * SLAB)
    query_docs = query_docs.astype(jnp.float32)
    for row in range(n_dp):
        same = key_docs[:, row : row + 1] == query_docs[row : row + 1, :]
        bias[row] = jnp.where(same & in_order, 0.0, MASKED)

    def backward(chunk, kind, offset, core):
        src, dst = ((kg, kp), (vg, vp))[kind]
        rows = rows_of(chunk)
        return remote(
            src.at[rows, 2 * (REACH - offset) + core],
            dst.at[offset, rows, :, own_kcols],
            back_send.at[chunk, kind, 2 * offset + core],
            back_recv.at[chunk, kind, 2 * offset + s],
            device_at(place - offset, core),
        )

    def backward_sibling(chunk, kind):
        src, dst = ((kg, kp), (vg, vp))[kind]
        rows = rows_of(chunk)
        return remote(
            src.at[rows, 2 * REACH + 1 - s],
            dst.at[0, rows, :, own_kcols],
            back_send.at[chunk, kind, 0],
            back_recv.at[chunk, kind, s],
            sibling,
        )

    def out_over(chunk, kind):
        src, dst = ((ob, att), (gb, dq))[kind]
        rows = rows_of(chunk)
        return remote(
            src.at[rows, 1 - s], dst.at[rows, :, own_cols],
            out_send.at[chunk, kind], out_recv.at[chunk, kind], sibling,
        )

    def local_out_copy(chunk, which):
        rows = rows_of(chunk)
        if which < 2:
            src, dst = ((kg, kp), (vg, vp))[which]
            return pltpu.make_async_copy(
                src.at[rows, 2 * REACH + s], dst.at[0, rows, :, own_kcols], local_out.at[chunk, which]
            )
        src, dst = ((ob, att), (gb, dq))[which - 2]
        return pltpu.make_async_copy(
            src.at[rows, s], dst.at[rows, :, own_cols], local_out.at[chunk, which]
        )

    def send_backward(chunk, act):
        for offset in range(REACH, 0, -1):

            @pl.when(place - offset >= 0)
            def _():
                for kind in range(2):
                    for core in range(2):
                        act(backward(chunk, kind, offset, core))

        for kind in range(2):
            act(backward_sibling(chunk, kind))
            act(out_over(chunk, kind))

    def await_inputs(chunk):
        rows = rows_of(chunk)
        for copy in local_in_copies(chunk):
            copy.wait()
        for kind in range(2):
            src, dst = ((k, kw), (v, vw))[kind]
            slot = 2 * REACH + 1 - s
            pltpu.make_async_copy(
                src.at[rows, :, own_kcols], dst.at[rows, slot], fwd_recv.at[chunk, kind, slot]
            ).wait()
            src, dst = ((q, qb), (u, ub))[kind]
            pltpu.make_async_copy(
                src.at[rows, :, own_cols], dst.at[rows, 1 - s], half_recv.at[chunk, kind]
            ).wait()
        for offset in range(1, REACH + 1):

            @pl.when(place >= offset)
            def _():
                for kind in range(2):
                    src, dst = ((k, kw), (v, vw))[kind]
                    for core in range(2):
                        slot = 2 * (REACH - offset) + core
                        pltpu.make_async_copy(
                            src.at[rows, :, own_kcols], dst.at[rows, slot], fwd_recv.at[chunk, kind, slot]
                        ).wait()

    def dot(a, b, dims):
        return lax.dot_general(a, b, (dims, ((), ())), preferred_element_type=jnp.float32)

    def compute(chunk):
        tasks = [(i, g) for i in range(CHUNK_ROWS) for g in range(2)]
        first = chunk * CHUNK_ROWS

        def stacked(ref, i, g):
            parts = []
            for h in range(GROUP):
                at = (g * GROUP + h) * HEAD_DIMENSION
                parts.append(ref[first + i, :, :, at : at + HEAD_DIMENSION].reshape(2 * SLAB, HEAD_DIMENSION))
            return jnp.concatenate(parts, axis=0)

        def windowed(ref, i, g):
            at = g * HEAD_DIMENSION
            return ref[first + i, :, :, at : at + HEAD_DIMENSION].reshape(WINDOW, HEAD_DIMENSION)

        def spread(ref, i, g, value):
            for h in range(GROUP):
                at = (g * GROUP + h) * HEAD_DIMENSION
                part = value[h * 2 * SLAB : (h + 1) * 2 * SLAB].astype(jnp.bfloat16)
                ref[first + i, :, :, at : at + HEAD_DIMENSION] = part.reshape(2, SLAB, HEAD_DIMENSION)

        def unwindow(ref, i, g, value):
            at = g * HEAD_DIMENSION
            ref[first + i, :, :, at : at + HEAD_DIMENSION] = value.astype(jnp.bfloat16).reshape(
                SLOTS, SLAB, HEAD_DIMENSION
            )

        scores = [dot(windowed(kw, i, g), stacked(qb, i, g), ((1,), (1,))) for i, g in tasks]
        prob_grads = [dot(windowed(vw, i, g), stacked(ub, i, g), ((1,), (1,))) for i, g in tasks]
        probs, grads = [], []
        for (i, g), score, prob_grad in zip(tasks, scores, prob_grads):
            score = score * SCALING + bias[first + i]
            weights = jnp.exp(score - jnp.max(score, axis=0, keepdims=True))
            normalized = weights / jnp.sum(weights, axis=0, keepdims=True)
            delta = jnp.sum(normalized * prob_grad, axis=0, keepdims=True)
            probs.append(normalized.astype(jnp.bfloat16))
            grads.append((normalized * (prob_grad - delta)).astype(jnp.bfloat16))
        for (i, g), prob, grad in zip(tasks, probs, grads):
            unwindow(kg, i, g, dot(grad, stacked(qb, i, g), ((1,), (0,))) * SCALING)
            unwindow(vg, i, g, dot(prob, stacked(ub, i, g), ((1,), (0,))))
        for (i, g), prob, grad in zip(tasks, probs, grads):
            spread(ob, i, g, dot(prob, windowed(vw, i, g), ((0,), (0,))))
            spread(gb, i, g, dot(grad, windowed(kw, i, g), ((0,), (0,))) * SCALING)

    def step(chunk, carry):
        await_inputs(chunk)

        @pl.when(chunk + AHEAD < CHUNKS)
        def _():
            send_forward(chunk + AHEAD, lambda copy: copy.start())

        compute(chunk)
        send_backward(chunk, lambda copy: copy.start())
        for which in range(4):
            local_out_copy(chunk, which).start()
        return carry

    lax.fori_loop(0, CHUNKS, step, 0)

    def finish(chunk, carry):
        rows = rows_of(chunk)
        for kind in range(2):
            local_out_copy(chunk, kind).wait()
            src, dst = ((kg, kp), (vg, vp))[kind]
            pltpu.make_async_copy(
                src.at[rows, 2 * REACH + 1 - s], dst.at[0, rows, :, sib_kcols], back_recv.at[chunk, kind, 1 - s]
            ).wait()
        for offset in range(1, REACH + 1):

            @pl.when(place + offset <= last)
            def _():
                for kind in range(2):
                    src, dst = ((kg, kp), (vg, vp))[kind]
                    for core in range(2):
                        pltpu.make_async_copy(
                            src.at[rows, 2 * REACH],
                            dst.at[offset, rows, :, pl.ds(core * HALF_K, HALF_K)],
                            back_recv.at[chunk, kind, 2 * offset + core],
                        ).wait()

        for part, total, target, kind in ((kp, ks, dk, 0), (vp, vs, dv, 1)):
            value = part[0, rows].astype(jnp.float32)
            for offset in range(1, REACH + 1):
                value += part[offset, rows].astype(jnp.float32)
            total[rows] = value.astype(jnp.bfloat16)
            pltpu.make_async_copy(total.at[rows], target.at[rows], final_out.at[chunk, kind]).start()
        return carry

    lax.fori_loop(0, CHUNKS, finish, 0)

    for step in range(1, n_dp):
        doc_near(step).wait_send()

    @pl.when(z < n_seq - 1)
    def _():
        for other in range(n_dp):
            doc_next(other).wait_send()

    def drain(chunk, carry):
        rows = rows_of(chunk)
        send_forward(chunk, lambda copy: copy.wait_send())
        send_backward(chunk, lambda copy: copy.wait_send())
        for kind in range(2):
            src, dst = ((ob, att), (gb, dq))[kind]
            pltpu.make_async_copy(
                src.at[rows, s], dst.at[rows, :, sib_cols], out_recv.at[chunk, kind]
            ).wait()
            local_out_copy(chunk, 2 + kind).wait()
            total, target = ((ks, dk), (vs, dv))[kind]
            pltpu.make_async_copy(total.at[rows], target.at[rows], final_out.at[chunk, kind]).wait()
        return carry

    lax.fori_loop(0, CHUNKS, drain, 0)


def store(att, dq, dk, dv, att_out, dq_out, dk_out, dv_out, done):
    pairs = ((att, att_out), (dq, dq_out), (dk, dk_out), (dv, dv_out))
    copies = [pltpu.make_async_copy(src, dst, done.at[i]) for i, (src, dst) in enumerate(pairs)]
    for copy in copies:
        copy.start()
    for copy in copies:
        copy.wait()


def direct(n_dp, n_seq, queries, keys, values, upstream, doc_ids):
    wide = (ROWS, SLAB, QUERY_HEADS * HEAD_DIMENSION)
    narrow = (ROWS, SLAB, KEY_VALUE_HEADS * HEAD_DIMENSION)
    half = jnp.bfloat16
    anywhere = pl.BlockSpec(memory_space=pl.ANY)
    dma = pltpu.SemaphoreType.DMA
    results = pl.pallas_call(
        functools.partial(kernel, n_dp, n_seq),
        out_shape=[jax.ShapeDtypeStruct(shape, half) for shape in (wide, wide, narrow, narrow)],
        in_specs=[pl.BlockSpec(memory_space=pltpu.HBM)] * 5,
        out_specs=[anywhere] * 4,
        scratch_shapes=[
            pltpu.VMEM(wide, half),
            pltpu.VMEM(narrow, half),
            pltpu.VMEM(narrow, half),
            pltpu.VMEM(wide, half),
            pltpu.VMEM((1, n_dp * SLAB), jnp.int32),
            pltpu.VMEM((ROWS, 2, SLAB, HALF_Q), half),
            pltpu.VMEM((ROWS, 2, SLAB, HALF_Q), half),
            pltpu.VMEM((ROWS, SLOTS, SLAB, HALF_K), half),
            pltpu.VMEM((ROWS, SLOTS, SLAB, HALF_K), half),
            pltpu.VMEM((ROWS, 2, SLAB, HALF_Q), half),
            pltpu.VMEM((ROWS, 2, SLAB, HALF_Q), half),
            pltpu.VMEM((ROWS, SLOTS, SLAB, HALF_K), half),
            pltpu.VMEM((ROWS, SLOTS, SLAB, HALF_K), half),
            pltpu.VMEM((REACH + 1,) + narrow, half),
            pltpu.VMEM((REACH + 1,) + narrow, half),
            pltpu.VMEM(narrow, half),
            pltpu.VMEM(narrow, half),
            pltpu.VMEM((2 * n_dp, 1, n_dp * SLAB), jnp.int32),
            pltpu.VMEM((n_dp, 2 * n_dp * SLAB), jnp.int32),
            pltpu.VMEM((ROWS, WINDOW, 128), jnp.float32),
            dma((5,)),
            dma((2 * n_dp,)),
            dma((2 * n_dp,)),
            dma(()),
            dma((CHUNKS, 2, SLOTS)),
            dma((CHUNKS, 2, SLOTS)),
            dma((CHUNKS, 2)),
            dma((CHUNKS, 2)),
            dma((CHUNKS, 4)),
            dma((CHUNKS, 2, SLOTS)),
            dma((CHUNKS, 2, SLOTS)),
            dma((CHUNKS, 2)),
            dma((CHUNKS, 2)),
            dma((CHUNKS, 4)),
            dma((CHUNKS, 2)),
        ],
        compiler_params=pltpu.CompilerParams(
            collective_id=0, has_side_effects=True, vmem_limit_bytes=48 * 1024 * 1024
        ),
        cost_estimate=pl.CostEstimate(flops=10**9, bytes_accessed=10**7, transcendentals=10**6),
    )(
        *[
            pltpu.with_memory_space_constraint(array, pltpu.HBM)
            for array in (
                queries.reshape(wide), keys.reshape(narrow), values.reshape(narrow),
                upstream.reshape(wide), doc_ids,
            )
        ]
    )
    stored = pl.pallas_call(
        store,
        out_shape=[jax.ShapeDtypeStruct(shape, half) for shape in (wide, wide, narrow, narrow)],
        in_specs=[anywhere] * 4,
        out_specs=[pl.BlockSpec(memory_space=pltpu.HBM)] * 4,
        scratch_shapes=[dma((4,))],
        compiler_params=pltpu.CompilerParams(vmem_limit_bytes=4 * 1024 * 1024),
    )(*results)
    tokens = ROWS * SLAB
    return tuple(array.reshape(1, tokens, array.shape[-1]) for array in stored)


def arranged(n_dp, n_seq, queries, keys, values, upstream, doc_ids):
    tokens = queries.shape[1]
    slab = tokens // n_dp
    longest = n_seq * tokens // 8
    if n_dp == ROWS and slab == SLAB and longest <= 2 * REACH * SLAB:
        return direct(n_dp, n_seq, queries, keys, values, upstream, doc_ids)
    return shards(queries, keys, values, upstream, doc_ids)


def pick(mesh):
    return functools.partial(arranged, mesh.shape["dp"], mesh.shape["seq"])


def solution(mesh):
    in_specs = (
        P("dp", "seq", None),
        P("dp", "seq", None),
        P("dp", "seq", None),
        P("dp", "seq", None),
        P("dp", "seq"),
    )
    out_specs = (
        P("dp", "seq", None),
        P("dp", "seq", None),
        P("dp", "seq", None),
        P("dp", "seq", None),
    )
    return jax.shard_map(
        pick(mesh), mesh=mesh, in_specs=in_specs, out_specs=out_specs, check_vma=False)
```

```python
import functools
import math

import jax
import jax.numpy as jnp
from jax import lax
from jax.experimental import pallas as pl
from jax.experimental.pallas import tpu as pltpu
from jax.sharding import PartitionSpec as P

QUERY_HEADS = 16
KEY_VALUE_HEADS = 4
HEAD_DIMENSION = 128


def attend(queries, keys, values, upstream, doc_row):
    seq_rows = queries.shape[0]
    scaling = 1.0 / math.sqrt(queries.shape[2])
    block_rows = min(512, seq_rows)
    longest = seq_rows // 8
    positions = lax.iota(jnp.int32, seq_rows)
    key_gradient = jnp.zeros(keys.shape, jnp.float32)
    value_gradient = jnp.zeros(values.shape, jnp.float32)
    attended_parts = []
    query_parts = []
    for number in range(seq_rows // block_rows):
        start_row = number * block_rows
        finish = start_row + block_rows
        lowest = max(0, start_row - longest)
        query_block = queries[start_row:finish]
        upstream_block = upstream[start_row:finish]
        key_part = keys[lowest:finish]
        value_part = values[lowest:finish]
        scores = (
            jnp.einsum("qhd,khd->hqk", query_block, key_part, preferred_element_type=jnp.float32)
            * scaling
        )
        allowed = (doc_row[None, lowest:finish] == doc_row[start_row:finish, None]) & (
            positions[None, lowest:finish] <= positions[start_row:finish, None]
        )
        scores = jnp.where(allowed[None], scores, -jnp.inf)
        largest = jnp.max(scores, axis=2, keepdims=True)
        weights = jnp.exp(scores - largest)
        normalized = weights / jnp.sum(weights, axis=2, keepdims=True)
        probs_half = normalized.astype(jnp.bfloat16)
        attended_block = jnp.einsum(
            "hqk,khd->qhd", probs_half, value_part, preferred_element_type=jnp.float32
        ).astype(jnp.bfloat16)
        row_delta = jnp.sum(
            upstream_block.astype(jnp.float32) * attended_block.astype(jnp.float32), axis=2
        ).T[:, :, None]
        prob_grad = jnp.einsum(
            "qhd,khd->hqk", upstream_block, value_part, preferred_element_type=jnp.float32
        )
        score_grad = (normalized * (prob_grad - row_delta)).astype(jnp.bfloat16)
        query_parts.append(
            (
                jnp.einsum("hqk,khd->qhd", score_grad, key_part, preferred_element_type=jnp.float32)
                * scaling
            ).astype(jnp.bfloat16)
        )
        key_gradient = key_gradient.at[lowest:finish].add(
            jnp.einsum("hqk,qhd->khd", score_grad, query_block, preferred_element_type=jnp.float32)
            * scaling
        )
        value_gradient = value_gradient.at[lowest:finish].add(
            jnp.einsum(
                "hqk,qhd->khd", probs_half, upstream_block, preferred_element_type=jnp.float32
            )
        )
        attended_parts.append(attended_block)
    return (
        jnp.concatenate(attended_parts),
        jnp.concatenate(query_parts),
        key_gradient,
        value_gradient,
    )


def shards(queries, keys, values, upstream, doc_ids):
    tokens_per_shard = queries.shape[1]
    group_count = lax.axis_size("dp")
    packed_slab_rows = tokens_per_shard // group_count
    head_local = QUERY_HEADS // lax.axis_size("seq")
    queries_per_group = QUERY_HEADS // KEY_VALUE_HEADS
    query_rows, key_row_array, value_row_array, upstream_rows = (
        lax.all_to_all(
            queries.reshape(group_count, packed_slab_rows, QUERY_HEADS * HEAD_DIMENSION),
            "dp",
            split_axis=0,
            concat_axis=0,
            tiled=True,
        ),
        lax.all_to_all(
            keys.reshape(group_count, packed_slab_rows, KEY_VALUE_HEADS * HEAD_DIMENSION),
            "dp",
            split_axis=0,
            concat_axis=0,
            tiled=True,
        ),
        lax.all_to_all(
            values.reshape(group_count, packed_slab_rows, KEY_VALUE_HEADS * HEAD_DIMENSION),
            "dp",
            split_axis=0,
            concat_axis=0,
            tiled=True,
        ),
        lax.all_to_all(
            upstream.reshape(group_count, packed_slab_rows, QUERY_HEADS * HEAD_DIMENSION),
            "dp",
            split_axis=0,
            concat_axis=0,
            tiled=True,
        ),
    )
    query_tok = query_rows.reshape(tokens_per_shard, QUERY_HEADS, HEAD_DIMENSION)
    upstream_tok = upstream_rows.reshape(tokens_per_shard, QUERY_HEADS, HEAD_DIMENSION)
    key_tokens = key_row_array.reshape(tokens_per_shard, KEY_VALUE_HEADS, HEAD_DIMENSION)
    value_tokens = value_row_array.reshape(tokens_per_shard, KEY_VALUE_HEADS, HEAD_DIMENSION)
    doc_row = lax.all_gather(doc_ids, "seq", axis=1, tiled=True)[0]
    query_head_array, incoming_gradient_heads = (
        lax.all_to_all(query_tok, "seq", split_axis=1, concat_axis=0, tiled=True),
        lax.all_to_all(upstream_tok, "seq", split_axis=1, concat_axis=0, tiled=True),
    )
    key_whole, value_whole = (
        lax.all_gather(key_tokens, "seq", axis=0, tiled=True),
        lax.all_gather(value_tokens, "seq", axis=0, tiled=True),
    )
    head_ids = (
        lax.axis_index("seq") * head_local + lax.iota(jnp.int32, head_local)
    ) // queries_per_group
    key_head_array = jnp.take(key_whole, head_ids, axis=1)
    value_head_array = jnp.take(value_whole, head_ids, axis=1)
    attended, query_grad, key_gradient, value_gradient = attend(
        query_head_array, key_head_array, value_head_array, incoming_gradient_heads, doc_row
    )
    attended_back, query_back = (
        lax.all_to_all(attended, "seq", split_axis=0, concat_axis=1, tiled=True),
        lax.all_to_all(query_grad, "seq", split_axis=0, concat_axis=1, tiled=True),
    )
    key_backward, value_backward = (
        lax.all_to_all(key_gradient, "seq", split_axis=0, concat_axis=1, tiled=True),
        lax.all_to_all(value_gradient, "seq", split_axis=0, concat_axis=1, tiled=True),
    )
    key_gradient_total = jnp.sum(
        key_backward.reshape(tokens_per_shard, KEY_VALUE_HEADS, queries_per_group, HEAD_DIMENSION),
        axis=2,
    ).astype(jnp.bfloat16)
    value_gradient_total = jnp.sum(
        value_backward.reshape(
            tokens_per_shard, KEY_VALUE_HEADS, queries_per_group, HEAD_DIMENSION
        ),
        axis=2,
    ).astype(jnp.bfloat16)
    attended_out, query_out, key_result, value_result = (
        lax.all_to_all(
            attended_back.reshape(group_count, packed_slab_rows, QUERY_HEADS * HEAD_DIMENSION),
            "dp",
            split_axis=0,
            concat_axis=0,
            tiled=True,
        ),
        lax.all_to_all(
            query_back.reshape(group_count, packed_slab_rows, QUERY_HEADS * HEAD_DIMENSION),
            "dp",
            split_axis=0,
            concat_axis=0,
            tiled=True,
        ),
        lax.all_to_all(
            key_gradient_total.reshape(
                group_count, packed_slab_rows, KEY_VALUE_HEADS * HEAD_DIMENSION
            ),
            "dp",
            split_axis=0,
            concat_axis=0,
            tiled=True,
        ),
        lax.all_to_all(
            value_gradient_total.reshape(
                group_count, packed_slab_rows, KEY_VALUE_HEADS * HEAD_DIMENSION
            ),
            "dp",
            split_axis=0,
            concat_axis=0,
            tiled=True,
        ),
    )
    return (
        attended_out.reshape(1, tokens_per_shard, QUERY_HEADS * HEAD_DIMENSION),
        query_out.reshape(1, tokens_per_shard, QUERY_HEADS * HEAD_DIMENSION),
        key_result.reshape(1, tokens_per_shard, KEY_VALUE_HEADS * HEAD_DIMENSION),
        value_result.reshape(1, tokens_per_shard, KEY_VALUE_HEADS * HEAD_DIMENSION),
    )


MESH = pl.DeviceIdType.MESH
SLAB = 16
ROWS = 8
CHUNKS = 4
AHEAD = 2
CHUNK_ROWS = ROWS // CHUNKS
REACH = 2
SLOTS = 2 * REACH + 2
WINDOW = SLOTS * SLAB
HALF_Q = QUERY_HEADS * HEAD_DIMENSION // 2
HALF_K = KEY_VALUE_HEADS * HEAD_DIMENSION // 2
GROUP = QUERY_HEADS // KEY_VALUE_HEADS
SCALING = 1.0 / math.sqrt(HEAD_DIMENSION)
MASKED = -1e30


def kernel(
    n_dp, n_seq, q_in, k_in, v_in, u_in, doc_in, att, dq, dk, dv,
    q, k, v, u, doc, qb, ub, kw, vw, ob, gb, kg, vg, kp, vp, ks, vs, docs, dwin, bias,
    staged, doc_send, doc_recv, doc_local, fwd_send, fwd_recv, half_send, half_recv, local_in,
    back_send, back_recv, out_send, out_recv, local_out, final_out,
):
    d = lax.axis_index("dp")
    z = lax.axis_index("seq")
    chip, s = d // 2, d % 2
    chips = n_dp // 2
    place = z * chips + chip
    last = n_seq * chips - 1
    before, after = (z + n_seq - 1) % n_seq, (z + 1) % n_seq
    sibling = (chip * 2 + 1 - s, z)

    def remote(src, dst, send, recv, device):
        return pltpu.make_async_remote_copy(
            src_ref=src, dst_ref=dst, send_sem=send, recv_sem=recv,
            device_id=device, device_id_type=MESH,
        )

    def device_at(where, core):
        inside = (where + n_seq * chips) % (n_seq * chips)
        return ((inside % chips) * 2 + core, inside // chips)

    stages = [
        pltpu.make_async_copy(src, dst, staged.at[i])
        for i, (src, dst) in enumerate(((doc_in, doc), (k_in, k), (v_in, v), (q_in, q), (u_in, u)))
    ]
    for copy in stages:
        copy.start()

    barrier = pltpu.get_barrier_semaphore()
    for step in range(1, n_dp):
        pl.semaphore_signal(barrier, inc=1, device_id=((d + step) % n_dp, z), device_id_type=MESH)

    @pl.when(z > 0)
    def _():
        for other in range(n_dp):
            pl.semaphore_signal(barrier, inc=1, device_id=(other, before), device_id_type=MESH)

    @pl.when(z < n_seq - 1)
    def _():
        for other in range(n_dp):
            pl.semaphore_signal(barrier, inc=1, device_id=(other, after), device_id_type=MESH)

    planes = (z > 0).astype(jnp.int32) + (z < n_seq - 1).astype(jnp.int32)
    own_cols = pl.ds(pl.multiple_of(s * HALF_Q, HALF_Q), HALF_Q)
    sib_cols = pl.ds(pl.multiple_of((1 - s) * HALF_Q, HALF_Q), HALF_Q)
    own_kcols = pl.ds(pl.multiple_of(s * HALF_K, HALF_K), HALF_K)
    sib_kcols = pl.ds(pl.multiple_of((1 - s) * HALF_K, HALF_K), HALF_K)

    def rows_of(chunk):
        return pl.ds(chunk * CHUNK_ROWS, CHUNK_ROWS)

    def local_in_copies(chunk):
        rows = rows_of(chunk)
        return [
            pltpu.make_async_copy(k.at[rows, :, own_kcols], kw.at[rows, 2 * REACH + s], local_in.at[chunk, 0]),
            pltpu.make_async_copy(v.at[rows, :, own_kcols], vw.at[rows, 2 * REACH + s], local_in.at[chunk, 1]),
            pltpu.make_async_copy(q.at[rows, :, own_cols], qb.at[rows, s], local_in.at[chunk, 2]),
            pltpu.make_async_copy(u.at[rows, :, own_cols], ub.at[rows, s], local_in.at[chunk, 3]),
        ]

    for offset in range(1, REACH + 1):

        @pl.when(place < offset)
        def _():
            for core in range(2):
                slot = 2 * (REACH - offset) + core
                kw[:, slot] = jnp.zeros((ROWS, SLAB, HALF_K), jnp.bfloat16)
                vw[:, slot] = jnp.zeros((ROWS, SLAB, HALF_K), jnp.bfloat16)

        @pl.when(place + offset > last)
        def _():
            kp[offset] = jnp.zeros((ROWS, SLAB, 2 * HALF_K), jnp.bfloat16)
            vp[offset] = jnp.zeros((ROWS, SLAB, 2 * HALF_K), jnp.bfloat16)

    @pl.when(z == 0)
    def _():
        docs[0:n_dp] = jnp.zeros((n_dp, 1, n_dp * SLAB), jnp.int32)

    pl.semaphore_wait(barrier, n_dp - 1 + n_dp * planes)

    stages[0].wait()
    own_doc = pltpu.make_async_copy(doc, docs.at[n_dp + d], doc_local)
    own_doc.start()

    def doc_near(step):
        return remote(
            doc, docs.at[n_dp + d], doc_send.at[step], doc_recv.at[n_dp + d], ((d + step) % n_dp, z)
        )

    def doc_next(other):
        return remote(
            doc, docs.at[d], doc_send.at[n_dp + other], doc_recv.at[d], (other, after)
        )

    for step in range(1, n_dp):
        doc_near(step).start()

    @pl.when(z < n_seq - 1)
    def _():
        for other in range(n_dp):
            doc_next(other).start()

    def forward(chunk, kind, offset, core):
        src, dst = ((k, kw), (v, vw))[kind]
        rows = rows_of(chunk)
        columns = pl.ds(core * HALF_K, HALF_K)
        return remote(
            src.at[rows, :, columns],
            dst.at[rows, 2 * (REACH - offset) + s],
            fwd_send.at[chunk, kind, 2 * offset + core],
            fwd_recv.at[chunk, kind, 2 * (REACH - offset) + s],
            device_at(place + offset, core),
        )

    def forward_sibling(chunk, kind):
        src, dst = ((k, kw), (v, vw))[kind]
        rows = rows_of(chunk)
        return remote(
            src.at[rows, :, sib_kcols],
            dst.at[rows, 2 * REACH + s],
            fwd_send.at[chunk, kind, 0],
            fwd_recv.at[chunk, kind, 2 * REACH + s],
            sibling,
        )

    def half_over(chunk, kind):
        src, dst = ((q, qb), (u, ub))[kind]
        rows = rows_of(chunk)
        return remote(
            src.at[rows, :, sib_cols], dst.at[rows, s],
            half_send.at[chunk, kind], half_recv.at[chunk, kind], sibling,
        )

    def send_far(chunk, act):
        for offset in range(REACH, 0, -1):

            @pl.when(place + offset <= last)
            def _():
                for kind in range(2):
                    for core in range(2):
                        act(forward(chunk, kind, offset, core))

    def send_near(chunk, act):
        for kind in range(2):
            act(forward_sibling(chunk, kind))
            act(half_over(chunk, kind))

    for copy in stages[1:3]:
        copy.wait()
    for chunk in range(AHEAD):
        send_far(chunk, lambda copy: copy.start())
    for copy in stages[3:]:
        copy.wait()
    for chunk in range(CHUNKS):
        send_near(chunk, lambda copy: copy.start())
        for copy in local_in_copies(chunk):
            copy.start()

    own_doc.wait()
    for step in range(1, n_dp):
        other = (d + step) % n_dp
        pltpu.make_async_copy(doc, docs.at[n_dp + other], doc_recv.at[n_dp + other]).wait()

    @pl.when(z > 0)
    def _():
        for other in range(n_dp):
            pltpu.make_async_copy(doc, docs.at[other], doc_recv.at[other]).wait()

    for row in range(n_dp):
        dwin[row : row + 1, 0:128] = docs[row]
        dwin[row : row + 1, 128:256] = docs[n_dp + row]
    lead = 128 - 2 * REACH * SLAB
    both = dwin[...]
    window = jnp.zeros((n_dp, 128), jnp.int32)
    for candidate in range(chips):
        begin = lead + candidate * 2 * SLAB
        shifted = pltpu.roll(both, 256 - begin, axis=1)[:, :128]
        window = jnp.where(chip == candidate, shifted, window)
    own = window[:, 2 * REACH * SLAB : WINDOW]
    query_docs = jnp.concatenate([own] * GROUP, axis=1)
    key_docs = window.astype(jnp.float32).T[:WINDOW]
    key_at = lax.broadcasted_iota(jnp.int32, (WINDOW, 128), 0)
    query_at = lax.broadcasted_iota(jnp.int32, (WINDOW, 128), 1) % (2 * SLAB) + 2 * REACH * SLAB
    in_order = (key_at <= query_at) & (key_at >= 2 * REACH * SLAB - place * 2 * SLAB)
    query_docs = query_docs.astype(jnp.float32)
    for row in range(n_dp):
        same = key_docs[:, row : row + 1] == query_docs[row : row + 1, :]
        bias[row] = jnp.where(same & in_order, 0.0, MASKED)

    def backward(chunk, kind, offset, core):
        src, dst = ((kg, kp), (vg, vp))[kind]
        rows = rows_of(chunk)
        return remote(
            src.at[rows, 2 * (REACH - offset) + core],
            dst.at[offset, rows, :, own_kcols],
            back_send.at[chunk, kind, 2 * offset + core],
            back_recv.at[chunk, kind, 2 * offset + s],
            device_at(place - offset, core),
        )

    def backward_sibling(chunk, kind):
        src, dst = ((kg, kp), (vg, vp))[kind]
        rows = rows_of(chunk)
        return remote(
            src.at[rows, 2 * REACH + 1 - s],
            dst.at[0, rows, :, own_kcols],
            back_send.at[chunk, kind, 0],
            back_recv.at[chunk, kind, s],
            sibling,
        )

    def out_over(chunk, kind):
        src, dst = ((ob, att), (gb, dq))[kind]
        rows = rows_of(chunk)
        return remote(
            src.at[rows, 1 - s], dst.at[rows, :, own_cols],
            out_send.at[chunk, kind], out_recv.at[chunk, kind], sibling,
        )

    def local_out_copy(chunk, which):
        rows = rows_of(chunk)
        if which < 2:
            src, dst = ((kg, kp), (vg, vp))[which]
            return pltpu.make_async_copy(
                src.at[rows, 2 * REACH + s], dst.at[0, rows, :, own_kcols], local_out.at[chunk, which]
            )
        src, dst = ((ob, att), (gb, dq))[which - 2]
        return pltpu.make_async_copy(
            src.at[rows, s], dst.at[rows, :, own_cols], local_out.at[chunk, which]
        )

    def send_backward(chunk, act):
        for offset in range(REACH, 0, -1):

            @pl.when(place - offset >= 0)
            def _():
                for kind in range(2):
                    for core in range(2):
                        act(backward(chunk, kind, offset, core))

        for kind in range(2):
            act(backward_sibling(chunk, kind))
            act(out_over(chunk, kind))

    def await_inputs(chunk):
        rows = rows_of(chunk)
        for copy in local_in_copies(chunk):
            copy.wait()
        for kind in range(2):
            src, dst = ((k, kw), (v, vw))[kind]
            slot = 2 * REACH + 1 - s
            pltpu.make_async_copy(
                src.at[rows, :, own_kcols], dst.at[rows, slot], fwd_recv.at[chunk, kind, slot]
            ).wait()
            src, dst = ((q, qb), (u, ub))[kind]
            pltpu.make_async_copy(
                src.at[rows, :, own_cols], dst.at[rows, 1 - s], half_recv.at[chunk, kind]
            ).wait()
        for offset in range(1, REACH + 1):

            @pl.when(place >= offset)
            def _():
                for kind in range(2):
                    src, dst = ((k, kw), (v, vw))[kind]
                    for core in range(2):
                        slot = 2 * (REACH - offset) + core
                        pltpu.make_async_copy(
                            src.at[rows, :, own_kcols], dst.at[rows, slot], fwd_recv.at[chunk, kind, slot]
                        ).wait()

    def dot(a, b, dims):
        return lax.dot_general(a, b, (dims, ((), ())), preferred_element_type=jnp.float32)

    def compute(chunk):
        tasks = [(i, g) for i in range(CHUNK_ROWS) for g in range(2)]
        first = chunk * CHUNK_ROWS

        def stacked(ref, i, g):
            parts = []
            for h in range(GROUP):
                at = (g * GROUP + h) * HEAD_DIMENSION
                parts.append(ref[first + i, :, :, at : at + HEAD_DIMENSION].reshape(2 * SLAB, HEAD_DIMENSION))
            return jnp.concatenate(parts, axis=0)

        def windowed(ref, i, g):
            at = g * HEAD_DIMENSION
            return ref[first + i, :, :, at : at + HEAD_DIMENSION].reshape(WINDOW, HEAD_DIMENSION)

        def spread(ref, i, g, value):
            for h in range(GROUP):
                at = (g * GROUP + h) * HEAD_DIMENSION
                part = value[h * 2 * SLAB : (h + 1) * 2 * SLAB].astype(jnp.bfloat16)
                ref[first + i, :, :, at : at + HEAD_DIMENSION] = part.reshape(2, SLAB, HEAD_DIMENSION)

        def unwindow(ref, i, g, value):
            at = g * HEAD_DIMENSION
            ref[first + i, :, :, at : at + HEAD_DIMENSION] = value.astype(jnp.bfloat16).reshape(
                SLOTS, SLAB, HEAD_DIMENSION
            )

        scores = [dot(windowed(kw, i, g), stacked(qb, i, g), ((1,), (1,))) for i, g in tasks]
        prob_grads = [dot(windowed(vw, i, g), stacked(ub, i, g), ((1,), (1,))) for i, g in tasks]
        probs, grads = [], []
        for (i, g), score, prob_grad in zip(tasks, scores, prob_grads):
            score = score * SCALING + bias[first + i]
            weights = jnp.exp(score - jnp.max(score, axis=0, keepdims=True))
            normalized = weights / jnp.sum(weights, axis=0, keepdims=True)
            delta = jnp.sum(normalized * prob_grad, axis=0, keepdims=True)
            probs.append(normalized.astype(jnp.bfloat16))
            grads.append((normalized * (prob_grad - delta)).astype(jnp.bfloat16))
        for (i, g), prob, grad in zip(tasks, probs, grads):
            unwindow(kg, i, g, dot(grad, stacked(qb, i, g), ((1,), (0,))) * SCALING)
            unwindow(vg, i, g, dot(prob, stacked(ub, i, g), ((1,), (0,))))
        for (i, g), prob, grad in zip(tasks, probs, grads):
            spread(ob, i, g, dot(prob, windowed(vw, i, g), ((0,), (0,))))
            spread(gb, i, g, dot(grad, windowed(kw, i, g), ((0,), (0,))) * SCALING)

    def step(chunk, carry):
        await_inputs(chunk)

        @pl.when(chunk + AHEAD < CHUNKS)
        def _():
            send_far(chunk + AHEAD, lambda copy: copy.start())

        compute(chunk)
        send_backward(chunk, lambda copy: copy.start())
        for which in range(4):
            local_out_copy(chunk, which).start()
        return carry

    lax.fori_loop(0, CHUNKS, step, 0)

    def finish(chunk, carry):
        rows = rows_of(chunk)
        for kind in range(2):
            local_out_copy(chunk, kind).wait()
            src, dst = ((kg, kp), (vg, vp))[kind]
            pltpu.make_async_copy(
                src.at[rows, 2 * REACH + 1 - s], dst.at[0, rows, :, sib_kcols], back_recv.at[chunk, kind, 1 - s]
            ).wait()
        for offset in range(1, REACH + 1):

            @pl.when(place + offset <= last)
            def _():
                for kind in range(2):
                    src, dst = ((kg, kp), (vg, vp))[kind]
                    for core in range(2):
                        pltpu.make_async_copy(
                            src.at[rows, 2 * REACH],
                            dst.at[offset, rows, :, pl.ds(core * HALF_K, HALF_K)],
                            back_recv.at[chunk, kind, 2 * offset + core],
                        ).wait()

        for part, total, target, kind in ((kp, ks, dk, 0), (vp, vs, dv, 1)):
            value = part[0, rows].astype(jnp.float32)
            for offset in range(1, REACH + 1):
                value += part[offset, rows].astype(jnp.float32)
            total[rows] = value.astype(jnp.bfloat16)
            pltpu.make_async_copy(total.at[rows], target.at[rows], final_out.at[chunk, kind]).start()
        return carry

    lax.fori_loop(0, CHUNKS, finish, 0)

    for step in range(1, n_dp):
        doc_near(step).wait_send()

    @pl.when(z < n_seq - 1)
    def _():
        for other in range(n_dp):
            doc_next(other).wait_send()

    def drain(chunk, carry):
        rows = rows_of(chunk)
        send_far(chunk, lambda copy: copy.wait_send())
        send_near(chunk, lambda copy: copy.wait_send())
        send_backward(chunk, lambda copy: copy.wait_send())
        for kind in range(2):
            src, dst = ((ob, att), (gb, dq))[kind]
            pltpu.make_async_copy(
                src.at[rows, s], dst.at[rows, :, sib_cols], out_recv.at[chunk, kind]
            ).wait()
            local_out_copy(chunk, 2 + kind).wait()
            total, target = ((ks, dk), (vs, dv))[kind]
            pltpu.make_async_copy(total.at[rows], target.at[rows], final_out.at[chunk, kind]).wait()
        return carry

    lax.fori_loop(0, CHUNKS, drain, 0)


def store(att, dq, dk, dv, att_out, dq_out, dk_out, dv_out, done):
    pairs = ((att, att_out), (dq, dq_out), (dk, dk_out), (dv, dv_out))
    copies = [pltpu.make_async_copy(src, dst, done.at[i]) for i, (src, dst) in enumerate(pairs)]
    for copy in copies:
        copy.start()
    for copy in copies:
        copy.wait()


def direct(n_dp, n_seq, queries, keys, values, upstream, doc_ids):
    wide = (ROWS, SLAB, QUERY_HEADS * HEAD_DIMENSION)
    narrow = (ROWS, SLAB, KEY_VALUE_HEADS * HEAD_DIMENSION)
    half = jnp.bfloat16
    anywhere = pl.BlockSpec(memory_space=pl.ANY)
    dma = pltpu.SemaphoreType.DMA
    results = pl.pallas_call(
        functools.partial(kernel, n_dp, n_seq),
        out_shape=[jax.ShapeDtypeStruct(shape, half) for shape in (wide, wide, narrow, narrow)],
        in_specs=[pl.BlockSpec(memory_space=pltpu.HBM)] * 5,
        out_specs=[anywhere] * 4,
        scratch_shapes=[
            pltpu.VMEM(wide, half),
            pltpu.VMEM(narrow, half),
            pltpu.VMEM(narrow, half),
            pltpu.VMEM(wide, half),
            pltpu.VMEM((1, n_dp * SLAB), jnp.int32),
            pltpu.VMEM((ROWS, 2, SLAB, HALF_Q), half),
            pltpu.VMEM((ROWS, 2, SLAB, HALF_Q), half),
            pltpu.VMEM((ROWS, SLOTS, SLAB, HALF_K), half),
            pltpu.VMEM((ROWS, SLOTS, SLAB, HALF_K), half),
            pltpu.VMEM((ROWS, 2, SLAB, HALF_Q), half),
            pltpu.VMEM((ROWS, 2, SLAB, HALF_Q), half),
            pltpu.VMEM((ROWS, SLOTS, SLAB, HALF_K), half),
            pltpu.VMEM((ROWS, SLOTS, SLAB, HALF_K), half),
            pltpu.VMEM((REACH + 1,) + narrow, half),
            pltpu.VMEM((REACH + 1,) + narrow, half),
            pltpu.VMEM(narrow, half),
            pltpu.VMEM(narrow, half),
            pltpu.VMEM((2 * n_dp, 1, n_dp * SLAB), jnp.int32),
            pltpu.VMEM((n_dp, 2 * n_dp * SLAB), jnp.int32),
            pltpu.VMEM((ROWS, WINDOW, 128), jnp.float32),
            dma((5,)),
            dma((2 * n_dp,)),
            dma((2 * n_dp,)),
            dma(()),
            dma((CHUNKS, 2, SLOTS)),
            dma((CHUNKS, 2, SLOTS)),
            dma((CHUNKS, 2)),
            dma((CHUNKS, 2)),
            dma((CHUNKS, 4)),
            dma((CHUNKS, 2, SLOTS)),
            dma((CHUNKS, 2, SLOTS)),
            dma((CHUNKS, 2)),
            dma((CHUNKS, 2)),
            dma((CHUNKS, 4)),
            dma((CHUNKS, 2)),
        ],
        compiler_params=pltpu.CompilerParams(
            collective_id=0, has_side_effects=True, vmem_limit_bytes=48 * 1024 * 1024
        ),
        cost_estimate=pl.CostEstimate(flops=10**9, bytes_accessed=10**7, transcendentals=10**6),
    )(
        *[
            pltpu.with_memory_space_constraint(array, pltpu.HBM)
            for array in (
                queries.reshape(wide), keys.reshape(narrow), values.reshape(narrow),
                upstream.reshape(wide), doc_ids,
            )
        ]
    )
    stored = pl.pallas_call(
        store,
        out_shape=[jax.ShapeDtypeStruct(shape, half) for shape in (wide, wide, narrow, narrow)],
        in_specs=[anywhere] * 4,
        out_specs=[pl.BlockSpec(memory_space=pltpu.HBM)] * 4,
        scratch_shapes=[dma((4,))],
        compiler_params=pltpu.CompilerParams(vmem_limit_bytes=4 * 1024 * 1024),
    )(*results)
    tokens = ROWS * SLAB
    return tuple(array.reshape(1, tokens, array.shape[-1]) for array in stored)


def arranged(n_dp, n_seq, queries, keys, values, upstream, doc_ids):
    tokens = queries.shape[1]
    slab = tokens // n_dp
    longest = n_seq * tokens // 8
    if n_dp == ROWS and slab == SLAB and longest <= 2 * REACH * SLAB:
        return direct(n_dp, n_seq, queries, keys, values, upstream, doc_ids)
    return shards(queries, keys, values, upstream, doc_ids)


def pick(mesh):
    return functools.partial(arranged, mesh.shape["dp"], mesh.shape["seq"])


def solution(mesh):
    in_specs = (
        P("dp", "seq", None),
        P("dp", "seq", None),
        P("dp", "seq", None),
        P("dp", "seq", None),
        P("dp", "seq"),
    )
    out_specs = (
        P("dp", "seq", None),
        P("dp", "seq", None),
        P("dp", "seq", None),
        P("dp", "seq", None),
    )
    return jax.shard_map(
        pick(mesh), mesh=mesh, in_specs=in_specs, out_specs=out_specs, check_vma=False)
```
